32 devices in a mesh: row: 8 (over z, x), col: 4 (over y, core).
Axes of the slice: x: 2, y: 2, z: 4, core: 2. Of those that a mesh axis runs over, the one named last changes fastest.
Arguments:
- descriptors: float32 [512, 64], P(('row', 'col')), may hold values from -6 to 6, as said below
- preference: float32 [512], P(('row', 'col')), may hold values from -4 to -0.5
- responsibility: float32 [512, 512], P('row', 'col'), may hold values from -6 to 4, as said below
- availability: float32 [512, 512], P('row', 'col'), may hold values from -2 to 0, as said below
Outputs:
- resp_out: float32 [512, 512], P('row', 'col')
- avail_out: float32 [512, 512], P('row', 'col')
The draws below stay inside these ranges and needn't reach their ends.
Inputs may be any that keep to these rules, and one draw needn't show every extreme that they name: `descriptors`: descriptors 64 m + 1, 64 m + 2 and 64 m + 3 are exact copies of descriptor 64 m (where they exist); the others are independent. `responsibility`: mostly negative; positive entries are rare and scattered over the columns. `availability`: columns 64 m + 1, 64 m + 2 and 64 m + 3 are exact copies of column 64 m (where they exist); the other entries are independent.
All inputs are finite; a program needn't handle non-finite values.
Results may differ from the reference program's by a relative error of at most 0.0003.
Values sent between devices are 32-bit elements; how exact they have to be, the bound alone decides.
A program may use at most 64 MiB of HBM per device.

```python
import jax
import jax.numpy as jnp
from jax import lax

WIDTH = 64
ITERS = 3
POINTS = 512


def group_source():
    index_line = jnp.arange(POINTS, dtype=jnp.int32)
    offset = index_line % 64
    return jnp.where(offset < 4, index_line - offset, index_line)


def draw_descriptors(key, part):
    base_key = jax.random.fold_in(key, 29)
    base = jnp.clip(jax.random.normal(base_key, (POINTS, WIDTH), jnp.float32), -6.0, 6.0)
    return base[group_source()]


def draw_availability(key, part):
    base_key = jax.random.fold_in(key, 31)
    base = jax.random.uniform(base_key, (POINTS, POINTS), jnp.float32, -2.0, 0.0)
    return base[:, group_source()]


def draw_responsibility(key, part):
    base_key = jax.random.fold_in(key, 17)
    key_base, key_bump, key_pick = jax.random.split(base_key, 3)
    base = -jax.random.uniform(key_base, (POINTS, POINTS), jnp.float32, 0.5, 4.0)
    bump = jax.random.uniform(key_bump, (POINTS, POINTS), jnp.float32, 0.5, 4.0)
    picked = jax.random.randint(key_pick, (POINTS, POINTS), 0, POINTS) < 3
    return jnp.where(picked, bump, base)


def level_of(stream_key, dims, cuts, smallest, high):
    factor_of, own = 1.0, jax.random.fold_in(stream_key, 6)
    for axis_at, shards_of in cuts:
        heights = jnp.exp(jax.random.uniform(jax.random.fold_in(own, axis_at), (shards_of,), jnp.float32, smallest / len(cuts), high / len(cuts)))
        factor_of = factor_of * jnp.repeat(heights, dims[axis_at] // shards_of).reshape([-1 if axis == axis_at else 1 for axis in range(len(dims))])
    return factor_of


def setup_inputs(seed: int = 0) -> dict:
    key_of = jax.random.split(jax.random.key(seed), 5)
    descriptors = draw_descriptors(jax.random.fold_in(key_of[4], 71), 0)
    preference = jnp.clip(-4.0 + 3.5 * jax.random.uniform(key_of[1], (POINTS,), jnp.float32) ** level_of(key_of[1], (POINTS,), ((0, 32),), -0.2, 0.2), -4.0, -0.5)
    responsibility = draw_responsibility(jax.random.fold_in(key_of[4], 71), 0)
    availability = draw_availability(jax.random.fold_in(key_of[4], 71), 0)
    return {"descriptors": descriptors, "preference": preference, "responsibility": responsibility, "availability": availability}


DAMP = 0.5
NEG_FILL = -1.0e30


def reference(descriptors, preference, responsibility, availability):
    norms = jnp.sum(descriptors * descriptors, 1)
    cross = jnp.dot(descriptors, descriptors.T, precision=lax.Precision.HIGHEST, preferred_element_type=jnp.float32)
    similarity = (2.0 * cross - norms[:, None] - norms[None, :]) / WIDTH
    index_line = jnp.arange(POINTS, dtype=jnp.int32)
    diag_mask = index_line[:, None] == index_line[None, :]
    similarity = jnp.where(diag_mask, preference[:, None], similarity)
    resp_now = responsibility
    avail_now = availability
    for step_index in range(ITERS):
        summed = avail_now + similarity
        best = jnp.max(summed, 1)
        at_best = summed == best[:, None]
        hits = jnp.sum(at_best, 1, dtype=jnp.float32)
        below = jnp.max(jnp.where(at_best, NEG_FILL, summed), 1)
        runner = jnp.where(hits >= 2.0, best, below)
        excluded = jnp.where(at_best, runner[:, None], best[:, None])
        resp_now = DAMP * resp_now + (1.0 - DAMP) * (similarity - excluded)
        kept = jnp.where(diag_mask, resp_now, jnp.maximum(resp_now, 0.0))
        column = jnp.sum(kept, 0)
        fresh = column[None, :] - kept
        fresh = jnp.where(diag_mask, fresh, jnp.minimum(fresh, 0.0))
        avail_now = DAMP * avail_now + (1.0 - DAMP) * fresh
    return resp_now, avail_now
```

```python
import functools

import jax
import jax.numpy as jnp
from jax import lax
from jax.experimental import pallas as pl
from jax.experimental.pallas import tpu as pltpu
from jax.sharding import PartitionSpec as P

ITERS = 3
DAMP = 0.5
NEG_FILL = -1e30
MESH = pl.DeviceIdType.MESH


def _loop(count, body):
    if count <= 4:
        for at in range(count):
            body(at)
    else:
        lax.fori_loop(0, count, lambda at, carry: (body(at), carry)[1], 0)


def _kernel(
    nr, nc, chunk,
    desc, pref, rin, ain, rout, aout,
    D, prefs, R, A, S, part, got, total,
    d1_send, d1_recv, d2_send, d2_recv, p_send, p_recv, a_send, a_recv,
    r_send, r_recv, c_send, l_send, c_recv,
):
    row, col = lax.axis_index("row"), lax.axis_index("col")
    points, width = desc.shape
    rows, cols = rin.shape
    span = cols // rows
    row_peers = [(lax.rem(row + d, nr), col) for d in range(1, nr)]
    col_peers = [(row, lax.rem(col + d, nc)) for d in range(1, nc)]

    def send(src, dst, send_sem, recv_sem, peer):
        pltpu.make_async_remote_copy(
            src_ref=src, dst_ref=dst, send_sem=send_sem, recv_sem=recv_sem,
            device_id=peer, device_id_type=MESH,
        ).start()

    def drain(ref, sem):
        pltpu.make_async_copy(ref, ref, sem).wait()

    barrier = pltpu.get_barrier_semaphore()
    for peer in row_peers + col_peers:
        pl.semaphore_signal(barrier, inc=1, device_id=peer, device_id_type=MESH)
    D[row, col] = desc[...]
    prefs[col] = pref[...]
    A[col] = ain[...]
    R[col] = rin[...]
    pl.semaphore_wait(barrier, nr + nc - 2)

    for peer in row_peers:
        send(desc, D.at[row, col], d1_send, d1_recv, peer)
    for peer in col_peers:
        send(ain, A.at[col], a_send, a_recv, peer)
    for peer in col_peers:
        send(pref, prefs.at[col], p_send, p_recv, peer)
    drain(D.at[pl.ds(0, nr - 1), 0], d1_recv)
    for peer in col_peers:
        send(D.at[:, col], D.at[:, col], d2_send, d2_recv, peer)
    for peer in col_peers:
        send(rin, R.at[col], r_send, r_recv, peer)
    drain(prefs.at[pl.ds(0, nc - 1)], p_recv)
    drain(D.at[:, pl.ds(0, nc - 1)], d2_recv)

    def diagonal(block, start, count):
        i = lax.broadcasted_iota(jnp.int32, (count, cols), 0) + (row * rows + start)
        k = lax.broadcasted_iota(jnp.int32, (count, cols), 1) + block * cols
        return i == k

    mine = D[row].reshape(rows, width)
    norm_mine = jnp.sum(mine * mine, 1, keepdims=True)
    pick = (
        lax.broadcasted_iota(jnp.int32, (points, points), 0)
        == lax.broadcasted_iota(jnp.int32, (points, points), 1)
    )
    own_pref = jnp.concatenate(
        [
            jnp.sum(jnp.where(pick, prefs[q], 0.0), 1, keepdims=True)
            for q in range(nc)
        ],
        0,
    )
    contract = (((1,), (1,)), ((), ()))

    def make_similarity(block):
        theirs = D[pl.ds(block * span, span)].reshape(cols, width)
        cross = lax.dot_general(
            mine, theirs, contract,
            precision=lax.Precision.HIGHEST, preferred_element_type=jnp.float32,
        )
        norm = lax.dot_general(
            jnp.ones((8, width), jnp.float32), theirs * theirs, contract,
            precision=lax.Precision.HIGHEST, preferred_element_type=jnp.float32,
        )[0:1]
        value = (2.0 * cross - norm_mine - norm) * (1.0 / width)
        S[block] = jnp.where(diagonal(block, 0, rows), own_pref, value)

    _loop(nc, make_similarity)
    drain(A.at[pl.ds(0, nc - 1)], a_recv)

    for step in range(ITERS):
        last = step == ITERS - 1
        if rows != chunk:
            part[step] = jnp.zeros((nc, cols), jnp.float32)

        def messages(at):
            start = at * chunk
            view = pl.ds(start, chunk)
            summed = [A[q, view] + S[q, view] for q in range(nc)]
            first, second = summed[0], None
            for value in summed[1:]:
                low = jnp.minimum(first, value)
                second = low if second is None else jnp.maximum(second, low)
                first = jnp.maximum(first, value)
            best = jnp.max(first, 1, keepdims=True)
            hits, below = None, None
            for value in summed:
                at_best = value == best
                hit = jnp.where(at_best, 1.0, 0.0)
                low = jnp.where(at_best, NEG_FILL, value)
                hits = hit if hits is None else hits + hit
                below = low if below is None else jnp.maximum(below, low)
            hits = jnp.sum(hits, 1, keepdims=True)
            below = jnp.max(below, 1, keepdims=True)
            runner = jnp.where(hits >= 2.0, best, below)
            if step == 0 and rows == chunk:
                drain(R.at[pl.ds(0, nc - 1)], r_recv)

            def respond(q):
                similarity = S[q, view]
                excluded = jnp.where(A[q, view] + similarity == best, runner, best)
                now = DAMP * R[q, view] + (1.0 - DAMP) * (similarity - excluded)
                R[q, view] = now
                kept = jnp.where(
                    diagonal(q, start, chunk), now, jnp.maximum(now, 0.0)
                )
                amount = jnp.sum(kept, 0, keepdims=True)
                if rows != chunk:
                    amount = amount + part[step, pl.ds(q, 1)]
                part[step, pl.ds(q, 1)] = amount

            if last:
                respond(col)
            else:
                for q in range(nc):
                    respond(q)

        if step == 0 and rows != chunk:
            drain(R.at[pl.ds(0, nc - 1)], r_recv)
        _loop(rows // chunk, messages)

        if last:
            for d, peer in enumerate(row_peers):
                send(
                    part.at[step, pl.ds(col, 1)], got.at[step, d, pl.ds(0, 1)],
                    l_send, c_recv.at[step], peer,
                )
            drain(got.at[step, :, pl.ds(0, 1)], c_recv.at[step])
            column = part[step, pl.ds(col, 1)]
            for d in range(nr - 1):
                column = column + got[step, d, 0:1]
            total[0:1] = column
        else:
            for d, peer in enumerate(row_peers):
                send(part.at[step], got.at[step, d], c_send, c_recv.at[step], peer)
            drain(got.at[step], c_recv.at[step])
            column = part[step]
            for d in range(nr - 1):
                column = column + got[step, d]
            total[...] = column

        def available(q, at, where_sum):
            start = at * chunk
            view = pl.ds(start, chunk)
            now = R[q, view]
            mask = diagonal(q, start, chunk)
            kept = jnp.where(mask, now, jnp.maximum(now, 0.0))
            fresh = total[where_sum] - kept
            fresh = jnp.where(mask, fresh, jnp.minimum(fresh, 0.0))
            return DAMP * A[q, view] + (1.0 - DAMP) * fresh

        def update(at):
            for q in range(nc):
                A[q, pl.ds(at * chunk, chunk)] = available(q, at, pl.ds(q, 1))

        def finish(at):
            view = pl.ds(at * chunk, chunk)
            rout[view] = R[col, view]
            aout[view] = available(col, at, pl.ds(0, 1))

        _loop(rows // chunk, finish if last else update)

    drain(D.at[pl.ds(0, nr - 1), 0], d1_send)
    drain(D.at[:, pl.ds(0, nc - 1)], d2_send)
    drain(prefs.at[pl.ds(0, nc - 1)], p_send)
    drain(A.at[pl.ds(0, nc - 1)], a_send)
    drain(R.at[pl.ds(0, nc - 1)], r_send)
    drain(got.at[pl.ds(0, ITERS - 1)], c_send)
    drain(got.at[ITERS - 1, :, pl.ds(0, 1)], l_send)


def _local(nr, nc, desc, pref, resp, avail):
    points, width = desc.shape
    rows, cols = resp.shape
    chunk = max(8, min(rows, 32768 // (nc * cols)))
    block = (nc, rows, cols)
    f32 = jnp.float32
    vmem = pl.BlockSpec(memory_space=pltpu.VMEM)
    dma = pltpu.SemaphoreType.DMA
    return pl.pallas_call(
        functools.partial(_kernel, nr, nc, chunk),
        out_shape=[jax.ShapeDtypeStruct((rows, cols), f32)] * 2,
        in_specs=[vmem] * 4,
        out_specs=[vmem] * 2,
        scratch_shapes=[
            pltpu.VMEM((nr, nc, points, width), f32),
            pltpu.VMEM((nc, 1, points), f32),
            pltpu.VMEM(block, f32),
            pltpu.VMEM(block, f32),
            pltpu.VMEM(block, f32),
            pltpu.VMEM((ITERS, nc, cols), f32),
            pltpu.VMEM((ITERS, nr - 1, nc, cols), f32),
            pltpu.VMEM((nc, cols), f32),
        ]
        + [dma] * 12
        + [dma((ITERS,))],
        compiler_params=pltpu.CompilerParams(
            collective_id=0, has_side_effects=True,
            vmem_limit_bytes=(48 if rows > 64 else 16) * 2**20,
        ),
    )(desc, pref.reshape(1, points), resp, avail)


def solution(mesh):
    placed = (P(("row", "col"), None), P(("row", "col")), P("row", "col"), P("row", "col"))
    return jax.shard_map(
        functools.partial(_local, mesh.shape["row"], mesh.shape["col"]),
        mesh=mesh,
        in_specs=placed,
        out_specs=(P("row", "col"), P("row", "col")),
        check_vma=False,
    )
```

```python
import functools

import jax
import jax.numpy as jnp
from jax import lax
from jax.experimental import pallas as pl
from jax.experimental.pallas import tpu as pltpu
from jax.sharding import PartitionSpec as P

ITERS = 3
DAMP = 0.5
NEG_FILL = -1e30
MESH = pl.DeviceIdType.MESH


def _loop(count, body):
    if count <= 4:
        for at in range(count):
            body(at)
    else:
        lax.fori_loop(0, count, lambda at, carry: (body(at), carry)[1], 0)


def _kernel(
    nr, nc, chunk,
    desc, pref, rin, ain, rout, aout,
    D, prefs, R, A, S, part, got, total,
    d_send, d_recv, p_send, p_recv, a_send, a_recv, r_send, r_recv,
    c_send, l_send, c_recv, f_send, f_recv,
):
    row, col = lax.axis_index("row"), lax.axis_index("col")
    ny = nc // 2
    y, core = col // 2, lax.rem(col, 2)
    points, width = desc.shape
    rows, cols = rin.shape
    span = cols // rows
    row_peers = [(lax.rem(row + d, nr), col) for d in range(1, nr)]
    y_peers = [(row, lax.rem(y + e, ny) * 2 + core) for e in range(1, ny)]
    far_peers = [
        (lax.rem(row + d, nr), lax.rem(y + e, ny) * 2 + core)
        for d in range(1, nr)
        for e in range(1, ny)
    ]
    sibling = (row, y * 2 + 1 - core)

    def send(src, dst, send_sem, recv_sem, peer):
        pltpu.make_async_remote_copy(
            src_ref=src, dst_ref=dst, send_sem=send_sem, recv_sem=recv_sem,
            device_id=peer, device_id_type=MESH,
        ).start()

    def drain(ref, sem):
        pltpu.make_async_copy(ref, ref, sem).wait()

    barrier = pltpu.get_barrier_semaphore()
    greeted = far_peers + row_peers + y_peers + [sibling]
    for peer in greeted:
        pl.semaphore_signal(barrier, inc=1, device_id=peer, device_id_type=MESH)
    for src, dst, sem in [
        (desc, D.at[row, y, core], d_recv), (ain, A.at[y, core], a_recv),
        (pref, prefs.at[y, core], p_recv), (rin, R.at[y, core], r_recv),
    ]:
        pltpu.make_async_copy(src, dst, sem).start()
    pl.semaphore_wait(barrier, len(greeted))

    for peer in far_peers + row_peers + y_peers:
        send(desc, D.at[row, y, core], d_send, d_recv, peer)
    for peer in y_peers:
        send(ain, A.at[y, core], a_send, a_recv, peer)
    for peer in y_peers:
        send(pref, prefs.at[y, core], p_send, p_recv, peer)
    for peer in y_peers:
        send(rin, R.at[y, core], r_send, r_recv, peer)

    def forward(at, ref):
        view = ref.at[:, :, core] if len(ref.shape) == 5 else ref.at[:, core]
        send(view, view, f_send.at[at], f_recv.at[at], sibling)

    drain(A.at[:, 0], a_recv)
    forward(0, A)
    drain(prefs.at[:, 0], p_recv)
    forward(1, prefs)
    drain(D.at[:, :, 0], d_recv)
    forward(2, D)
    drain(R.at[:, 0], r_recv)
    forward(3, R)
    drain(prefs.at[:, 0], f_recv.at[1])
    drain(D.at[:, :, 0], f_recv.at[2])

    def diagonal(block, start, count):
        i = lax.broadcasted_iota(jnp.int32, (count, cols), 0) + (row * rows + start)
        k = lax.broadcasted_iota(jnp.int32, (count, cols), 1) + block * cols
        return i == k

    mine = D[row].reshape(rows, width)
    norm_mine = jnp.sum(mine * mine, 1, keepdims=True)
    pick = (
        lax.broadcasted_iota(jnp.int32, (points, points), 0)
        == lax.broadcasted_iota(jnp.int32, (points, points), 1)
    )
    own_pref = jnp.concatenate(
        [
            jnp.sum(jnp.where(pick, prefs[q // 2, q % 2], 0.0), 1, keepdims=True)
            for q in range(nc)
        ],
        0,
    )
    contract = (((1,), (1,)), ((), ()))

    def make_similarity(block):
        theirs = D[pl.ds(block * span, span)].reshape(cols, width)
        cross = lax.dot_general(
            mine, theirs, contract,
            precision=lax.Precision.HIGHEST, preferred_element_type=jnp.float32,
        )
        norm = lax.dot_general(
            jnp.ones((8, width), jnp.float32), theirs * theirs, contract,
            precision=lax.Precision.HIGHEST, preferred_element_type=jnp.float32,
        )[0:1]
        value = (2.0 * cross - norm_mine - norm) * (1.0 / width)
        S[block] = jnp.where(diagonal(block, 0, rows), own_pref, value)

    _loop(nc, make_similarity)
    drain(A.at[:, 0], f_recv.at[0])

    for step in range(ITERS):
        last = step == ITERS - 1
        if rows != chunk:
            part[step] = jnp.zeros((nc, cols), jnp.float32)

        def messages(at):
            start = at * chunk
            view = pl.ds(start, chunk)
            summed = [A[q // 2, lax.rem(q, 2), view] + S[q, view] for q in range(nc)]
            first, second = summed[0], None
            for value in summed[1:]:
                low = jnp.minimum(first, value)
                second = low if second is None else jnp.maximum(second, low)
                first = jnp.maximum(first, value)
            best = jnp.max(first, 1, keepdims=True)
            hits, below = None, None
            for value in summed:
                at_best = value == best
                hit = jnp.where(at_best, 1.0, 0.0)
                low = jnp.where(at_best, NEG_FILL, value)
                hits = hit if hits is None else hits + hit
                below = low if below is None else jnp.maximum(below, low)
            hits = jnp.sum(hits, 1, keepdims=True)
            below = jnp.max(below, 1, keepdims=True)
            runner = jnp.where(hits >= 2.0, best, below)
            if step == 0 and rows == chunk:
                drain(R.at[:, 0], f_recv.at[3])
                drain(R.at[:, 0], f_send.at[3])

            def respond(q):
                similarity = S[q, view]
                excluded = jnp.where(A[q // 2, lax.rem(q, 2), view] + similarity == best, runner, best)
                now = DAMP * R[q // 2, lax.rem(q, 2), view] + (1.0 - DAMP) * (similarity - excluded)
                R[q // 2, lax.rem(q, 2), view] = now
                kept = jnp.where(
                    diagonal(q, start, chunk), now, jnp.maximum(now, 0.0)
                )
                amount = jnp.sum(kept, 0, keepdims=True)
                if rows != chunk:
                    amount = amount + part[step, pl.ds(q, 1)]
                part[step, pl.ds(q, 1)] = amount

            if last:
                respond(col)
            else:
                for q in range(nc):
                    respond(q)

        if step == 0 and rows != chunk:
            drain(R.at[:, 0], f_recv.at[3])
            drain(R.at[:, 0], f_send.at[3])
        _loop(rows // chunk, messages)

        if last:
            for d, peer in enumerate(row_peers):
                send(
                    part.at[step, pl.ds(col, 1)], got.at[step, d, pl.ds(0, 1)],
                    l_send, c_recv.at[step], peer,
                )
            drain(got.at[step, :, pl.ds(0, 1)], c_recv.at[step])
            column = part[step, pl.ds(col, 1)]
            for d in range(nr - 1):
                column = column + got[step, d, 0:1]
            total[0:1] = column
        else:
            for d, peer in enumerate(row_peers):
                send(part.at[step], got.at[step, d], c_send, c_recv.at[step], peer)
            drain(got.at[step], c_recv.at[step])
            column = part[step]
            for d in range(nr - 1):
                column = column + got[step, d]
            total[...] = column

        if step == 0:
            drain(A.at[:, 0], f_send.at[0])

        def available(q, at, where_sum):
            start = at * chunk
            view = pl.ds(start, chunk)
            now = R[q // 2, lax.rem(q, 2), view]
            mask = diagonal(q, start, chunk)
            kept = jnp.where(mask, now, jnp.maximum(now, 0.0))
            fresh = total[where_sum] - kept
            fresh = jnp.where(mask, fresh, jnp.minimum(fresh, 0.0))
            return A[q // 2, lax.rem(q, 2), view] + fresh

        def update(at):
            for q in range(nc):
                A[q // 2, q % 2, pl.ds(at * chunk, chunk)] = DAMP * available(q, at, pl.ds(q, 1))

        def finish(at):
            view = pl.ds(at * chunk, chunk)
            rout[view] = R[y, core, view] * 2.0
            aout[view] = available(col, at, pl.ds(0, 1))

        _loop(rows // chunk, finish if last else update)

    drain(D.at[pl.ds(0, nr - 1), :, 0], d_send)
    drain(D.at[0, pl.ds(0, ny - 1), 0], d_send)
    drain(prefs.at[pl.ds(0, ny - 1), 0], p_send)
    drain(A.at[pl.ds(0, ny - 1), 0], a_send)
    drain(R.at[pl.ds(0, ny - 1), 0], r_send)
    drain(prefs.at[:, 0], f_send.at[1])
    drain(D.at[:, :, 0], f_send.at[2])
    drain(got.at[pl.ds(0, ITERS - 1)], c_send)
    drain(got.at[ITERS - 1, :, pl.ds(0, 1)], l_send)


def _local(nr, nc, desc, pref, resp, avail):
    points, width = desc.shape
    rows, cols = resp.shape
    chunk = max(8, min(rows, 32768 // (nc * cols)))
    f32 = jnp.float32
    vmem = pl.BlockSpec(memory_space=pltpu.VMEM)
    dma = pltpu.SemaphoreType.DMA
    twice = pl.pallas_call(
        functools.partial(_kernel, nr, nc, chunk),
        out_shape=[jax.ShapeDtypeStruct((rows, cols), f32)] * 2,
        in_specs=[pl.BlockSpec(memory_space=pltpu.HBM)] * 4,
        out_specs=[vmem] * 2,
        scratch_shapes=[
            pltpu.VMEM((nr, nc // 2, 2, points, width), f32),
            pltpu.VMEM((nc // 2, 2, 1, points), f32),
            pltpu.VMEM((nc // 2, 2, rows, cols), f32),
            pltpu.VMEM((nc // 2, 2, rows, cols), f32),
            pltpu.VMEM((nc, rows, cols), f32),
            pltpu.VMEM((ITERS, nc, cols), f32),
            pltpu.VMEM((ITERS, nr - 1, nc, cols), f32),
            pltpu.VMEM((nc, cols), f32),
        ]
        + [dma] * 10
        + [dma((ITERS,))]
        + [dma((4,))] * 2,
        compiler_params=pltpu.CompilerParams(
            collective_id=0, has_side_effects=True,
            vmem_limit_bytes=60 * 2**20,
        ),
    )(desc, pref.reshape(1, points), resp, avail)
    return tuple(DAMP * value for value in twice)


def solution(mesh):
    placed = (P(("row", "col"), None), P(("row", "col")), P("row", "col"), P("row", "col"))
    return jax.shard_map(
        functools.partial(_local, mesh.shape["row"], mesh.shape["col"]),
        mesh=mesh,
        in_specs=placed,
        out_specs=(P("row", "col"), P("row", "col")),
        check_vma=False,
    )
```

```python
import functools

import jax
import jax.numpy as jnp
from jax import lax
from jax.experimental import pallas as pl
from jax.experimental.pallas import tpu as pltpu
from jax.sharding import PartitionSpec as P

ITERS = 3
DAMP = 0.5
NEG_FILL = -1e30
MESH = pl.DeviceIdType.MESH


def _loop(count, body):
    if count <= 4:
        for at in range(count):
            body(at)
    else:
        lax.fori_loop(0, count, lambda at, carry: (body(at), carry)[1], 0)


def _kernel(
    nr, nc, chunk,
    desc, pref, rin, ain, rout, aout,
    D, prefs, R, A, S, part, got, total,
    d_send, d_recv, p_send, p_recv, a_send, a_recv, r_send, r_recv,
    c_send, l_send, c_recv, f_send, f_recv,
):
    row, col = lax.axis_index("row"), lax.axis_index("col")
    ny = nc // 2
    y, core = col // 2, lax.rem(col, 2)
    points, width = desc.shape
    rows, cols = rin.shape
    span = cols // rows
    pair, side = row // 2, lax.rem(row, 2)
    wide = 2 * rows
    place = pl.ds(side * rows, rows)
    row_peers = [(lax.rem(row + d, nr), col) for d in range(1, nr)]
    y_peers = [(row, lax.rem(y + e, ny) * 2 + core) for e in range(1, ny)]
    near_peers = y_peers + [
        (pair * 2 + 1 - side, lax.rem(y + e, ny) * 2 + core) for e in range(ny)
    ]
    sum_peers = [(lax.rem(row + 2 * d, nr), col) for d in range(1, nr // 2)]
    far_peers = [
        (lax.rem(row + d, nr), lax.rem(y + e, ny) * 2 + core)
        for d in range(1, nr)
        for e in range(1, ny)
    ]
    sibling = (row, y * 2 + 1 - core)

    def send(src, dst, send_sem, recv_sem, peer):
        pltpu.make_async_remote_copy(
            src_ref=src, dst_ref=dst, send_sem=send_sem, recv_sem=recv_sem,
            device_id=peer, device_id_type=MESH,
        ).start()

    def drain(ref, sem):
        pltpu.make_async_copy(ref, ref, sem).wait()

    barrier = pltpu.get_barrier_semaphore()
    greeted = far_peers + row_peers + y_peers + [sibling]
    for peer in greeted:
        pl.semaphore_signal(barrier, inc=1, device_id=peer, device_id_type=MESH)
    for src, dst, sem in [
        (desc, D.at[row, y, core], d_recv), (ain, A.at[y, core, place], a_recv),
        (pref, prefs.at[side, y, core], p_recv),
        (rin, R.at[y, core, place], r_recv),
    ]:
        pltpu.make_async_copy(src, dst, sem).start()
    pl.semaphore_wait(barrier, len(greeted))

    for peer in far_peers + row_peers + y_peers:
        send(desc, D.at[row, y, core], d_send, d_recv, peer)
    for peer in near_peers:
        send(ain, A.at[y, core, place], a_send, a_recv, peer)
    for peer in near_peers:
        send(pref, prefs.at[side, y, core], p_send, p_recv, peer)
    for peer in near_peers:
        send(rin, R.at[y, core, place], r_send, r_recv, peer)

    def forward(at, ref):
        view = ref.at[:, core] if len(ref.shape) == 4 else ref.at[:, :, core]
        send(view, view, f_send.at[at], f_recv.at[at], sibling)

    drain(A.at[:, 0], a_recv)
    forward(0, A)
    drain(prefs.at[:, :, 0], p_recv)
    forward(1, prefs)
    drain(D.at[:, :, 0], d_recv)
    forward(2, D)
    drain(R.at[:, 0], r_recv)
    forward(3, R)
    drain(prefs.at[:, :, 0], f_recv.at[1])
    drain(D.at[:, :, 0], f_recv.at[2])

    def diagonal(block, start, count):
        i = lax.broadcasted_iota(jnp.int32, (count, cols), 0) + (pair * wide + start)
        k = lax.broadcasted_iota(jnp.int32, (count, cols), 1) + block * cols
        return i == k

    mine = D[pl.ds(pair * 2, 2)].reshape(wide, width)
    norm_mine = jnp.sum(mine * mine, 1, keepdims=True)
    pick = (
        lax.broadcasted_iota(jnp.int32, (points, points), 0)
        == lax.broadcasted_iota(jnp.int32, (points, points), 1)
    )
    own_pref = jnp.concatenate(
        [
            jnp.sum(jnp.where(pick, prefs[x, q // 2, q % 2], 0.0), 1, keepdims=True)
            for x in range(2)
            for q in range(nc)
        ],
        0,
    )
    contract = (((1,), (1,)), ((), ()))

    def make_similarity(block):
        theirs = D[pl.ds(block * span, span)].reshape(cols, width)
        cross = lax.dot_general(
            mine, theirs, contract,
            precision=lax.Precision.HIGHEST, preferred_element_type=jnp.float32,
        )
        norm = lax.dot_general(
            jnp.ones((8, width), jnp.float32), theirs * theirs, contract,
            precision=lax.Precision.HIGHEST, preferred_element_type=jnp.float32,
        )[0:1]
        value = (2.0 * cross - norm_mine - norm) * (1.0 / width)
        S[block] = jnp.where(diagonal(block, 0, wide), own_pref, value)

    _loop(nc, make_similarity)
    drain(A.at[:, 0], f_recv.at[0])

    for step in range(ITERS):
        last = step == ITERS - 1
        if wide != chunk:
            part[step] = jnp.zeros((nc, cols), jnp.float32)

        def messages(at):
            start = at * chunk
            view = pl.ds(start, chunk)
            summed = [A[q // 2, lax.rem(q, 2), view] + S[q, view] for q in range(nc)]
            first, second = summed[0], None
            for value in summed[1:]:
                low = jnp.minimum(first, value)
                second = low if second is None else jnp.maximum(second, low)
                first = jnp.maximum(first, value)
            best = jnp.max(first, 1, keepdims=True)
            hits, below = None, None
            for value in summed:
                at_best = value == best
                hit = jnp.where(at_best, 1.0, 0.0)
                low = jnp.where(at_best, NEG_FILL, value)
                hits = hit if hits is None else hits + hit
                below = low if below is None else jnp.maximum(below, low)
            hits = jnp.sum(hits, 1, keepdims=True)
            below = jnp.max(below, 1, keepdims=True)
            runner = jnp.where(hits >= 2.0, best, below)
            if step == 0 and type(at) is int and at == 0:
                drain(R.at[:, 0], f_recv.at[3])
                drain(R.at[:, 0], f_send.at[3])

            def respond(q):
                similarity = S[q, view]
                excluded = jnp.where(A[q // 2, lax.rem(q, 2), view] + similarity == best, runner, best)
                now = DAMP * R[q // 2, lax.rem(q, 2), view] + (1.0 - DAMP) * (similarity - excluded)
                R[q // 2, lax.rem(q, 2), view] = now
                kept = jnp.where(
                    diagonal(q, start, chunk), now, jnp.maximum(now, 0.0)
                )
                amount = jnp.sum(kept, 0, keepdims=True)
                if wide != chunk:
                    amount = amount + part[step, pl.ds(q, 1)]
                part[step, pl.ds(q, 1)] = amount

            if last:
                respond(col)
            else:
                for q in range(nc):
                    respond(q)

        if step == 0 and wide // chunk > 4:
            drain(R.at[:, 0], f_recv.at[3])
            drain(R.at[:, 0], f_send.at[3])
        _loop(wide // chunk, messages)

        if last:
            for d, peer in enumerate(sum_peers):
                send(
                    part.at[step, pl.ds(col, 1)], got.at[step, d, pl.ds(0, 1)],
                    l_send, c_recv.at[step], peer,
                )
            drain(got.at[step, :, pl.ds(0, 1)], c_recv.at[step])
            column = part[step, pl.ds(col, 1)]
            for d in range(nr // 2 - 1):
                column = column + got[step, d, 0:1]
            total[0:1] = column
        else:
            for d, peer in enumerate(sum_peers):
                send(part.at[step], got.at[step, d], c_send, c_recv.at[step], peer)
            drain(got.at[step], c_recv.at[step])
            column = part[step]
            for d in range(nr // 2 - 1):
                column = column + got[step, d]
            total[...] = column

        if step == 0:
            drain(A.at[:, 0], f_send.at[0])

        def available(q, at, where_sum):
            start = at * chunk
            view = pl.ds(start, chunk)
            now = R[q // 2, lax.rem(q, 2), view]
            mask = diagonal(q, start, chunk)
            kept = jnp.where(mask, now, jnp.maximum(now, 0.0))
            fresh = total[where_sum] - kept
            fresh = jnp.where(mask, fresh, jnp.minimum(fresh, 0.0))
            return A[q // 2, lax.rem(q, 2), view] + fresh

        def update(at):
            for q in range(nc):
                A[q // 2, q % 2, pl.ds(at * chunk, chunk)] = DAMP * available(q, at, pl.ds(q, 1))

        def finish(at):
            view = pl.ds(at * chunk, chunk)
            offset = at + side * (rows // chunk)
            rout[view] = R[y, core, pl.ds(offset * chunk, chunk)] * 2.0
            aout[view] = available(col, offset, pl.ds(0, 1))

        if last:
            _loop(rows // chunk, finish)
        else:
            _loop(wide // chunk, update)

    drain(D.at[pl.ds(0, nr - 1), :, 0], d_send)
    drain(D.at[0, pl.ds(0, ny - 1), 0], d_send)
    drain(prefs.at[0, pl.ds(0, ny - 1), 0], p_send)
    drain(prefs.at[1, :, 0], p_send)
    for ref, sem in ((A, a_send), (R, r_send)):
        drain(ref.at[pl.ds(0, ny - 1), 0], sem)
        drain(ref.at[0, 0, pl.ds(0, rows)], sem)
    drain(prefs.at[:, :, 0], f_send.at[1])
    drain(D.at[:, :, 0], f_send.at[2])
    drain(got.at[pl.ds(0, ITERS - 1)], c_send)
    drain(got.at[ITERS - 1, :, pl.ds(0, 1)], l_send)


def _local(nr, nc, desc, pref, resp, avail):
    points, width = desc.shape
    rows, cols = resp.shape
    chunk = max(8, min(rows, 32768 // (nc * cols)))
    f32 = jnp.float32
    vmem = pl.BlockSpec(memory_space=pltpu.VMEM)
    dma = pltpu.SemaphoreType.DMA
    twice = pl.pallas_call(
        functools.partial(_kernel, nr, nc, chunk),
        out_shape=[pltpu.VMEM((rows, cols), f32)] * 2,
        in_specs=[pl.BlockSpec(memory_space=pltpu.HBM)] * 4,
        out_specs=[vmem] * 2,
        scratch_shapes=[
            pltpu.VMEM((nr, nc // 2, 2, points, width), f32),
            pltpu.VMEM((2, nc // 2, 2, 1, points), f32),
            pltpu.VMEM((nc // 2, 2, 2 * rows, cols), f32),
            pltpu.VMEM((nc // 2, 2, 2 * rows, cols), f32),
            pltpu.VMEM((nc, 2 * rows, cols), f32),
            pltpu.VMEM((ITERS, nc, cols), f32),
            pltpu.VMEM((ITERS, nr // 2 - 1, nc, cols), f32),
            pltpu.VMEM((nc, cols), f32),
        ]
        + [dma] * 10
        + [dma((ITERS,))]
        + [dma((4,))] * 2,
        compiler_params=pltpu.CompilerParams(
            collective_id=0, has_side_effects=True,
            vmem_limit_bytes=60 * 2**20,
        ),
    )(desc, pref.reshape(1, points), resp, avail)
    return tuple(DAMP * value for value in twice)


def solution(mesh):
    placed = (P(("row", "col"), None), P(("row", "col")), P("row", "col"), P("row", "col"))
    return jax.shard_map(
        functools.partial(_local, mesh.shape["row"], mesh.shape["col"]),
        mesh=mesh,
        in_specs=placed,
        out_specs=(P("row", "col"), P("row", "col")),
        check_vma=False,
    )
```
